128 devices in a mesh: mom: 16 (over x, z_lo, core), tm: 8 (over z_hi, y).
Axes of the slice: x: 4, y: 4, z: 4 (z_hi: 2, z_lo: 2; z = z_hi * 2 + z_lo), core: 2. Of those that a mesh axis runs over, the one named last changes fastest.
Arguments:
- lesser: float32 [2, 256, 2, 2, 256, 256], P(None, 'mom', None, None, 'tm'), may hold values from -6 to 6
- greater: float32 [2, 256, 2, 2, 256, 256], P(None, 'mom', None, None, 'tm'), may hold values from -6 to 6
- site_of: int32 [256], replicated, may hold values from 0 to 255, as said below
Outputs:
- polarization: float32 [2, 256, 2, 2, 256, 256], P(None, 'mom', None, None, 'tm')
The draws below stay inside these ranges and needn't reach their ends.
Inputs may be any that keep to these rules, and one draw needn't show every extreme that they name: `site_of`: each of 0 to 255 appears once.
All inputs are finite; a program needn't handle non-finite values.
Results may differ from the reference program's by a relative error of at most 0.0003.
Values sent between devices are 32-bit elements; how exact they have to be, the bound alone decides.
No kernel may reach another device: no remote copies, remote signals or barrier semaphores. Data moves between devices by JAX's collectives and lax.ppermute only.
A program may use at most 128 MiB of HBM per device.

```python
import math
import jax
import jax.numpy as jnp
from jax import lax

L = 16
NO = 2
NT = 256
K = 256


def draw_site_of(key, part):
    key = jax.random.fold_in(key, 7)
    return jax.random.permutation(key, K).astype(jnp.int32)


def steps_of(stream_key, shape, shards, least, high):
    loudness, own = 1.0, jax.random.fold_in(stream_key, 6)
    for dim, shards_of in shards:
        heights = jnp.exp(jax.random.uniform(jax.random.fold_in(own, dim), (shards_of,), jnp.float32, least / len(shards), high / len(shards)))
        loudness = loudness * jnp.repeat(heights, shape[dim] // shards_of).reshape([-1 if axis == dim else 1 for axis in range(len(shape))])
    return loudness


def bell_draw(stream_key, extent, width, reach, split=(), kind=jnp.bfloat16):
    values = jax.random.normal(stream_key, extent, jnp.float32) * width
    if len(split) > 0:
        values = steps_of(stream_key, extent, split, -0.22, 0.18) * values
    return jnp.clip(values, min=-reach, max=reach).astype(kind)


def setup_inputs(seed: int = 0) -> dict:
    streams_of = jax.random.split(jax.random.key(seed), 4)
    return {
        "lesser": bell_draw(streams_of[0], (2, K, NO, NO, NT, NT), 1.0, 6.0, ((1, 16), (4, 8)), jnp.float32),
        "greater": bell_draw(streams_of[1], (2, K, NO, NO, NT, NT), 1.0, 6.0, ((1, 16), (4, 8)), jnp.float32),
        "site_of": draw_site_of(jax.random.fold_in(streams_of[3], 71), 0),
    }


def phase_tables(site_of):
    momenta = site_of.shape[0]
    lattice = jnp.arange(momenta, dtype=jnp.int32)
    turn_count = ((lattice // L)[:, None] * (site_of // L)[None, :] + (lattice % L)[:, None] * (site_of % L)[None, :]) % L
    angles = turn_count.astype(jnp.float32) * (2.0 * math.pi / L)
    scaling = 1.0 / math.sqrt(momenta)
    cosine = jnp.cos(angles) * scaling
    sine_part = jnp.sin(angles) * scaling
    forward = jnp.concatenate([jnp.concatenate([cosine, -sine_part], 1), jnp.concatenate([sine_part, cosine], 1)], 0)
    mirrored = jnp.concatenate([jnp.concatenate([cosine, sine_part], 1), jnp.concatenate([-sine_part, cosine], 1)], 0)
    backward = jnp.concatenate([jnp.concatenate([cosine.T, sine_part.T], 1), jnp.concatenate([-sine_part.T, cosine.T], 1)], 0)
    return (forward, mirrored, backward)

def transform(matrix, values):
    dims_in = values.shape
    flattened = values.reshape(dims_in[0] * dims_in[1], -1)
    return jnp.dot(matrix, flattened, precision=lax.Precision.HIGHEST).reshape(dims_in)

def bubble(lesser_disp, greater_disp):
    real_part = lesser_disp[0] * greater_disp[1] + lesser_disp[1] * greater_disp[0]
    imag_part = lesser_disp[1] * greater_disp[1] - lesser_disp[0] * greater_disp[0]
    return jnp.stack([real_part, imag_part])

def reference(lesser, greater, site_of):
    forward, mirrored, backward = phase_tables(site_of)
    block_rows = 32

    def one_block(block_index):
        row_start = (block_index * block_rows).astype(jnp.int32)
        lesser_rows = lax.dynamic_slice_in_dim(lesser, row_start, block_rows, 4)
        greater_cols = lax.dynamic_slice_in_dim(greater, row_start, block_rows, 5)
        turned = jnp.transpose(greater_cols, (0, 1, 3, 2, 5, 4))
        product = bubble(transform(forward, lesser_rows), transform(mirrored, turned))
        return transform(backward, product)
    blocks = lax.map(one_block, jnp.arange(NT // block_rows, dtype=jnp.int32))
    return jnp.moveaxis(blocks, 0, 4).reshape(lesser.shape)
```

```python
import math

import jax
import jax.numpy as jnp
from jax import lax
from jax.experimental import pallas as pl
from jax.experimental.pallas import tpu as pltpu
from jax.sharding import PartitionSpec as P

L = 16
VMEM = 48 * 1024 * 1024
F32 = jnp.float32
BF16 = jnp.bfloat16


def params():
    return pltpu.CompilerParams(vmem_limit_bytes=VMEM)


def phase_tables(site_of):
    momenta = site_of.shape[0]
    lattice = jnp.arange(momenta, dtype=jnp.int32)
    turn_count = (
        (lattice // L)[:, None] * (site_of // L)[None, :]
        + (lattice % L)[:, None] * (site_of % L)[None, :]
    ) % L
    angles = turn_count.astype(F32) * (2.0 * math.pi / L)
    scaling = 1.0 / math.sqrt(momenta)
    cosine = (jnp.cos(angles) * scaling).reshape(momenta, 16, 1, 16)
    sine = (jnp.sin(angles) * scaling).reshape(momenta, 16, 1, 16)
    forward = jnp.stack(
        [jnp.concatenate([cosine, -sine], 2), jnp.concatenate([sine, cosine], 2)], 0
    ).reshape(2 * momenta, 2 * momenta)
    mirrored = jnp.stack(
        [jnp.concatenate([cosine, sine], 2), jnp.concatenate([-sine, cosine], 2)], 0
    ).reshape(2 * momenta, 2 * momenta)
    return forward, mirrored, forward.T


def split(x):
    high = x.astype(BF16)
    return high, (x - high.astype(F32)).astype(BF16)


def load_time(ref, t):
    return jnp.concatenate([ref[pl.ds(8 * h + t, 512, stride=16), :] for h in range(2)], 1)


def store_table(table_ref, cat_ref):
    n = table_ref.shape[1]
    high, low = split(table_ref[...])
    cat_ref[:, 0:n] = high
    cat_ref[:, n : 2 * n] = high
    cat_ref[:, 2 * n : 3 * n] = low


def times(cat_ref, x):
    high, low = split(x)
    return jnp.dot(
        cat_ref[...], jnp.concatenate([high, low, high], 0), preferred_element_type=F32
    )


def pack_lesser_body(i_ref, o_ref):
    for g in range(4):
        for h in range(2):
            o_ref[g, 0, :, h] = i_ref[0, :, 0, 8 * g : 8 * g + 8, 128 * h : 128 * h + 128]


def pack_lesser(values):
    return pl.pallas_call(
        pack_lesser_body,
        grid=(2, 4),
        in_specs=[pl.BlockSpec((1, 16, 1, 32, 256), lambda c, o: (c, 0, o, 0, 0))],
        out_specs=pl.BlockSpec((4, 1, 16, 2, 8, 128), lambda c, o: (o, c, 0, 0, 0, 0)),
        out_shape=jax.ShapeDtypeStruct((16, 2, 16, 2, 8, 128), F32),
        compiler_params=params(),
    )(values)


def pack_greater_body(i_ref, o_ref):
    for q in range(4):
        for h in range(2):
            block = i_ref[0, 4 * q : 4 * q + 4, 0, :, 128 * h : 128 * h + 128]
            turned = block.reshape(128, 128).T
            for s in range(4):
                for g in range(4):
                    r = 32 * s + 8 * g
                    o_ref[0, g, 4 * h + s, 0, q] = turned[r : r + 8, :]


def pack_greater(values):
    return pl.pallas_call(
        pack_greater_body,
        grid=(2, 4),
        in_specs=[
            pl.BlockSpec((1, 16, 1, 32, 256), lambda c, o: (c, 0, (o % 2) * 2 + o // 2, 0, 0))
        ],
        out_specs=pl.BlockSpec((1, 4, 8, 1, 4, 8, 128), lambda c, o: (o, 0, 0, c, 0, 0, 0)),
        out_shape=jax.ShapeDtypeStruct((4, 4, 8, 2, 4, 8, 128), F32),
        compiler_params=params(),
    )(values)


def lesser_body(x_ref, table_ref, o_ref, cat_ref):
    t = pl.program_id(0)

    @pl.when(t == 0)
    def _():
        store_table(table_ref, cat_ref)

    o_ref[0] = times(cat_ref, load_time(x_ref, t))


def lesser_transform(rows, table):
    return pl.pallas_call(
        lesser_body,
        grid=(8,),
        in_specs=[
            pl.BlockSpec((8192, 128), lambda t: (0, 0)),
            pl.BlockSpec((512, 512), lambda t: (0, 0)),
        ],
        out_specs=pl.BlockSpec((1, 512, 256), lambda t: (t, 0, 0)),
        out_shape=jax.ShapeDtypeStruct((8, 512, 256), F32),
        scratch_shapes=[pltpu.VMEM((512, 1536), BF16)],
        compiler_params=params(),
        cost_estimate=pl.CostEstimate(
            flops=2 * 512 * 1536 * 2048, bytes_accessed=9 << 20, transcendentals=0
        ),
    )(rows, table)


def swap_blocks(tiles):
    lane = lax.broadcasted_iota(jnp.int32, tiles[0].shape, 1)
    a, b, c, d = tiles
    low = lane < 64
    pairs = []
    for p, q in ((a, c), (b, d)):
        pairs.append(jnp.where(low, p, pltpu.roll(q, 64, 1)))
        pairs.append(jnp.where(low, pltpu.roll(p, 64, 1), q))
    e, f, g, h = pairs[0], pairs[2], pairs[1], pairs[3]
    even = (lane // 32) % 2 == 0
    return (
        jnp.where(even, e, pltpu.roll(f, 32, 1)),
        jnp.where(even, pltpu.roll(e, 96, 1), f),
        jnp.where(even, g, pltpu.roll(h, 32, 1)),
        jnp.where(even, pltpu.roll(g, 96, 1), h),
    )


def bubble_body(x_ref, l_ref, mirrored_ref, backward_ref, o_ref, g_ref, mcat_ref, bcat_ref):
    t = pl.program_id(0)

    @pl.when(t == 0)
    def _():
        store_table(mirrored_ref, mcat_ref)
        store_table(backward_ref, bcat_ref)

        def shard(m, carry):
            for c in range(2):
                for h in range(2):
                    tiles = [x_ref[m, 4 * h + s, c].reshape(32, 128) for s in range(4)]
                    for k, tile in enumerate(swap_blocks(tiles)):
                        for q in range(4):
                            row = ((m * 2 + c) * 16 + 4 * q + k) * 16 + 8 * h
                            g_ref[pl.ds(pl.multiple_of(row, 8), 8), :] = tile[8 * q : 8 * q + 8]
            return carry

        lax.fori_loop(0, 16, shard, 0)

    greater = times(mcat_ref, load_time(g_ref, t))
    lr, li = l_ref[0, 0:256], l_ref[0, 256:512]
    gr, gi = greater[0:256], greater[256:512]
    product = jnp.concatenate([lr * gi + li * gr, li * gi - lr * gr], 0)
    result = times(bcat_ref, product)
    for h in range(2):
        o_ref[pl.ds(8 * h + t, 512, stride=16), :] = result[:, 128 * h : 128 * h + 128]


def bubble(greater, lesser_disp, mirrored, backward):
    return pl.pallas_call(
        bubble_body,
        grid=(8,),
        in_specs=[
            pl.BlockSpec((16, 8, 2, 4, 8, 128), lambda t: (0,) * 6),
            pl.BlockSpec((1, 512, 256), lambda t: (t, 0, 0)),
            pl.BlockSpec((512, 512), lambda t: (0, 0)),
            pl.BlockSpec((512, 512), lambda t: (0, 0)),
        ],
        out_specs=pl.BlockSpec((8192, 128), lambda t: (0, 0)),
        out_shape=jax.ShapeDtypeStruct((8192, 128), F32),
        scratch_shapes=[
            pltpu.VMEM((8192, 128), F32),
            pltpu.VMEM((512, 1536), BF16),
            pltpu.VMEM((512, 1536), BF16),
        ],
        compiler_params=params(),
        cost_estimate=pl.CostEstimate(
            flops=4 * 512 * 1536 * 2048, bytes_accessed=14 << 20, transcendentals=0
        ),
    )(greater, lesser_disp, mirrored, backward)


def unpack_body(i_ref, o_ref):
    for g in range(4):
        for h in range(2):
            o_ref[0, :, 0, 8 * g : 8 * g + 8, 128 * h : 128 * h + 128] = i_ref[g, 0, :, h]


def unpack(values):
    return pl.pallas_call(
        unpack_body,
        grid=(2, 4),
        in_specs=[pl.BlockSpec((4, 1, 16, 2, 8, 128), lambda c, o: (o, c, 0, 0, 0, 0))],
        out_specs=pl.BlockSpec((1, 16, 1, 32, 256), lambda c, o: (c, 0, o, 0, 0)),
        out_shape=jax.ShapeDtypeStruct((2, 16, 4, 32, 256), F32),
        compiler_params=params(),
    )(values)


def local(lesser, greater, site_of):
    shape = lesser.shape
    merged = (2, 16, 4, 32, 256)
    lesser_out = pack_lesser(lesser.reshape(merged)).reshape(16, 512, 128)
    lesser_rows = lax.all_to_all(lesser_out, "mom", 0, 0, tiled=True).reshape(8192, 128)
    greater_out = pack_greater(greater.reshape(merged)).reshape(128, 64, 128)
    greater_rows = lax.all_to_all(greater_out, ("mom", "tm"), 0, 0, tiled=True)
    forward, mirrored, backward = phase_tables(site_of)
    lesser_disp = lesser_transform(lesser_rows, forward)
    moved = bubble(greater_rows.reshape(16, 8, 2, 4, 8, 128), lesser_disp, mirrored, backward)
    back = lax.all_to_all(moved.reshape(16, 512, 128), "mom", 0, 0, tiled=True)
    return unpack(back.reshape(16, 2, 16, 2, 8, 128)).reshape(shape)


def solution(mesh):
    in_specs = (P(None, "mom", None, None, "tm", None), P(None, "mom", None, None, "tm", None), P())
    out_specs = P(None, "mom", None, None, "tm", None)
    return jax.shard_map(local, mesh=mesh, in_specs=in_specs, out_specs=out_specs, check_vma=False)
```

```python
import math

import jax
import jax.numpy as jnp
from jax import lax
from jax.experimental import pallas as pl
from jax.experimental.pallas import tpu as pltpu
from jax.sharding import PartitionSpec as P

L = 16
VMEM = 56 * 1024 * 1024
F32 = jnp.float32
BF16 = jnp.bfloat16
BLOCK = (2, 16, 8, 128)
ANY = pl.BlockSpec(memory_space=pl.ANY)
HBM = pl.BlockSpec(memory_space=pltpu.HBM)


def params():
    return pltpu.CompilerParams(vmem_limit_bytes=VMEM)


def cost():
    return pl.CostEstimate(flops=1, bytes_accessed=1, transcendentals=0)


def shape(*dims):
    return jax.ShapeDtypeStruct(dims, F32)


def split(x):
    high = x.astype(BF16)
    return high, (x - high.astype(F32)).astype(BF16)


def cosines(turns):
    turns = turns % L
    turns = jnp.where(turns > 8, L - turns, turns)
    near = jnp.where(turns > 4, 8 - turns, turns)
    value = jnp.zeros(turns.shape, F32)
    for step in range(4):
        value = jnp.where(near == step, math.cos(2.0 * math.pi * step / L) / L, value)
    return jnp.where(turns > 4, -value, value)


def phase_turns(lattice, site):
    return (lattice // L) * (site // L) + (lattice % L) * (site % L)


def table_body(lesser_ref, greater_ref, result_ref, *outs):
    rows = lax.broadcasted_iota(jnp.int32, (512, 512), 0)
    columns = lax.broadcasted_iota(jnp.int32, (512, 512), 1)
    forward = phase_turns(rows % 256, lesser_ref[...]) + 4 * ((columns // 16) % 2 - rows // 256)
    mirrored = phase_turns(rows % 256, greater_ref[...]) - 4 * ((columns // 4) % 2 - rows // 256)
    backward = phase_turns(columns % 256, result_ref[...]) + 4 * ((rows // 16) % 2 - columns // 256)
    for out, turns in zip(outs, (forward, mirrored, backward)):
        high, low = split(cosines(turns + L))
        out[:, 0:512] = high
        out[:, 512:1024] = low


def phase_tables(site_of):
    parts = jnp.broadcast_to(site_of.reshape(16, 1, 16), (16, 2, 16))
    columns = parts.reshape(512)
    quads = parts.reshape(16, 2, 4, 4).transpose(3, 0, 1, 2).reshape(1, 512)
    return pl.pallas_call(
        table_body,
        out_shape=(jax.ShapeDtypeStruct((512, 1024), BF16),) * 3,
        compiler_params=params(),
        cost_estimate=cost(),
    )(columns.reshape(1, 512), quads, columns.reshape(512, 1))


def times(table_ref, x):
    high, low = split(x)
    table_high, table_low = table_ref[:, 0:512], table_ref[:, 512:1024]
    product = jnp.dot(table_high, high, preferred_element_type=F32)
    product += jnp.dot(table_high, low, preferred_element_type=F32)
    return product + jnp.dot(table_low, high, preferred_element_type=F32)


def part(ref, m):
    return ref.at[:, :, m // 4, pl.ds(m % 4 * 8, 8), :]


def half(ref, m, h):
    return ref.at[m, :, :, :, pl.ds(128 * h, 128)]


def relay(loads, stores):
    for group in loads:
        for copy in group:
            copy.start()
    for group, after in zip(loads, stores):
        for copy in group:
            copy.wait()
        for copy in after:
            copy.start()
    for group in stores:
        for copy in group:
            copy.wait()


RELAY = [
    pltpu.VMEM((16, 2, 16, 8, 256), F32),
    pltpu.SemaphoreType.DMA((16,)),
    pltpu.SemaphoreType.DMA((16, 2)),
]


def pack_body(i_ref, o_ref, buffer, one, two):
    copy = pltpu.make_async_copy
    relay(
        [[copy(part(i_ref, m), buffer.at[m], one.at[m])] for m in range(16)],
        [
            [copy(half(buffer, m, h), o_ref.at[m, h], two.at[m, h]) for h in range(2)]
            for m in range(16)
        ],
    )


def pack(values):
    return pl.pallas_call(
        pack_body,
        in_specs=[HBM],
        out_specs=HBM,
        out_shape=shape(16, 2, *BLOCK),
        scratch_shapes=RELAY,
        compiler_params=params(),
        cost_estimate=cost(),
    )(values)


def unpack_body(i_ref, o_ref, buffer, one, two):
    copy = pltpu.make_async_copy
    relay(
        [
            [copy(i_ref.at[m, h], half(buffer, m, h), two.at[m, h]) for h in range(2)]
            for m in range(16)
        ],
        [[copy(buffer.at[m], part(o_ref, m), one.at[m])] for m in range(16)],
    )


def unpack(values):
    return pl.pallas_call(
        unpack_body,
        in_specs=[ANY],
        out_specs=HBM,
        out_shape=shape(2, 16, 4, 32, 256),
        scratch_shapes=RELAY,
        compiler_params=params(),
        cost_estimate=cost(),
    )(values)


def swap_rows(tiles):
    tiles = list(tiles)
    row = lax.broadcasted_iota(jnp.int32, tiles[0].shape, 1)
    for step in (4, 2, 1):
        keep = (row // step) % 2 == 0
        for i in range(8):
            if i // step % 2 == 0:
                a, b = tiles[i], tiles[i + step]
                tiles[i] = jnp.where(keep, a, pltpu.roll(b, step, 1))
                tiles[i + step] = jnp.where(keep, pltpu.roll(a, 8 - step, 1), b)
    return tiles


def pack_greater_body(i_ref, o_ref):
    for h in range(2):
        turned = []
        for c in range(2):
            for q in range(4):
                block = i_ref[c, 4 * q : 4 * q + 4, 0, :, 128 * h : 128 * h + 128]
                turned.append(block.reshape(128, 128).T.reshape(16, 8, 128))
        for t, tile in enumerate(swap_rows(turned)):
            for s in range(4):
                for g in range(4):
                    o_ref[0, g, 4 * h + s, t] = tile[4 * s + g]


def pack_greater(values):
    return pl.pallas_call(
        pack_greater_body,
        grid=(4,),
        in_specs=[
            pl.BlockSpec((2, 16, 1, 32, 256), lambda o: (0, 0, (o % 2) * 2 + o // 2, 0, 0))
        ],
        out_specs=pl.BlockSpec((1, 4, 8, 8, 8, 128), lambda o: (o, 0, 0, 0, 0, 0)),
        out_shape=shape(4, 4, 8, 8, 8, 128),
        compiler_params=params(),
        cost_estimate=cost(),
    )(values)


def swap_blocks(tiles):
    lane = lax.broadcasted_iota(jnp.int32, tiles[0].shape, 1)
    a, b, c, d = tiles
    low = lane < 64
    pairs = []
    for p, q in ((a, c), (b, d)):
        pairs.append(jnp.where(low, p, pltpu.roll(q, 64, 1)))
        pairs.append(jnp.where(low, pltpu.roll(p, 64, 1), q))
    e, f, g, h = pairs[0], pairs[2], pairs[1], pairs[3]
    even = (lane // 32) % 2 == 0
    return (
        jnp.where(even, e, pltpu.roll(f, 32, 1)),
        jnp.where(even, pltpu.roll(e, 96, 1), f),
        jnp.where(even, g, pltpu.roll(h, 32, 1)),
        jnp.where(even, pltpu.roll(g, 96, 1), h),
    )


ROWS = pl.BlockSpec((16, 1, 256, 128), lambda h, t: (0, h, 0, 0))
DISP = pl.BlockSpec((1, 1, 512, 256), lambda h, t: (h, t, 0, 0))
TABLE = pl.BlockSpec((512, 1024), lambda h, t: (0, 0))


def lesser_body(x_ref, table_ref, o_ref):
    step = pl.program_id(1)
    rows = x_ref.reshape(4096, 128)
    x = jnp.concatenate([rows[pl.ds(2 * step + i, 512, stride=8), :] for i in range(2)], 1)
    o_ref[0, 0] = times(table_ref, x)


def lesser_transform(rows, table):
    return pl.pallas_call(
        lesser_body,
        grid=(2, 4),
        in_specs=[ROWS, TABLE],
        out_specs=DISP,
        out_shape=shape(2, 4, 512, 256),
        compiler_params=params(),
        cost_estimate=cost(),
    )(rows, table)


def bubble(lesser, greater):
    lr, li = lesser[0:256], lesser[256:512]
    gr, gi = greater[0:256], greater[256:512]
    return jnp.concatenate([lr * gi + li * gr, li * gi - lr * gr], 0)


def bubble_body(x_ref, l_ref, mirrored_ref, backward_ref, o_ref, result_ref):
    step = pl.program_id(1)
    pairs = []
    for i in range(2):
        tiles = [x_ref[:, s, i].reshape(128, 128) for s in range(4)]
        pairs.append(jnp.concatenate(swap_blocks(tiles), 0))
    product = bubble(l_ref[0, 0], times(mirrored_ref, jnp.concatenate(pairs, 1)))
    result = times(backward_ref, product)
    for i in range(2):
        result_ref[2 * step + i] = result[:, 128 * i : 128 * i + 128]

    @pl.when(step == 3)
    def _():
        def shard(m, carry):
            row = pl.multiple_of(32 * m, 32)
            tiles = [result_ref[t, pl.ds(row, 32), :].reshape(4, 8, 128) for t in range(8)]
            o_ref[m, 0] = jnp.stack(swap_rows(tiles), 1).reshape(256, 128)
            return carry

        lax.fori_loop(0, 16, shard, 0)


def bubble_transform(greater, lesser_disp, mirrored, backward):
    return pl.pallas_call(
        bubble_body,
        grid=(2, 4),
        in_specs=[
            pl.BlockSpec((16, 4, 2, 8, 128), lambda h, t: (0, h, t, 0, 0)),
            DISP,
            TABLE,
            TABLE,
        ],
        out_specs=ROWS,
        out_shape=shape(16, 2, 256, 128),
        scratch_shapes=[pltpu.VMEM((8, 512, 128), F32)],
        compiler_params=params(),
        cost_estimate=cost(),
    )(greater, lesser_disp, mirrored, backward)


def local(lesser, greater, site_of):
    merged = (2, 16, 4, 32, 256)
    lesser_out = pack(lesser.reshape(merged)).reshape(16, 512, 128)
    lesser_rows = lax.all_to_all(lesser_out, "mom", 0, 0, tiled=True).reshape(16, 2, 256, 128)
    greater_out = pack_greater(greater.reshape(merged)).reshape(128, 64, 128)
    greater_rows = lax.all_to_all(greater_out, ("mom", "tm"), 0, 0, tiled=True)
    forward, mirrored, backward = phase_tables(site_of)
    disp = lesser_transform(lesser_rows, forward)
    moved = bubble_transform(greater_rows.reshape(16, 8, 8, 8, 128), disp, mirrored, backward)
    back = lax.all_to_all(moved.reshape(16, 512, 128), "mom", 0, 0, tiled=True)
    return unpack(back.reshape(16, 2, *BLOCK)).reshape(lesser.shape)


def solution(mesh):
    in_specs = (P(None, "mom", None, None, "tm", None), P(None, "mom", None, None, "tm", None), P())
    out_specs = P(None, "mom", None, None, "tm", None)
    return jax.shard_map(local, mesh=mesh, in_specs=in_specs, out_specs=out_specs, check_vma=False)
```

```python
import functools
import math

import jax
import jax.numpy as jnp
from jax import lax
from jax.experimental import pallas as pl
from jax.experimental.pallas import tpu as pltpu
from jax.sharding import PartitionSpec as P

L = 16
VMEM = 56 * 1024 * 1024
F32 = jnp.float32
BF16 = jnp.bfloat16
BLOCK = (2, 16, 8, 128)
ANY = pl.BlockSpec(memory_space=pl.ANY)
HBM = pl.BlockSpec(memory_space=pltpu.HBM)
SCALAR = pl.BlockSpec(memory_space=pltpu.SMEM)
DISTANCES = [(dz, dx, dc) for dz in range(2) for dx in range(4) for dc in range(2)]


def params():
    return pltpu.CompilerParams(vmem_limit_bytes=VMEM)


def cost():
    return pl.CostEstimate(flops=1, bytes_accessed=1, transcendentals=0)


def shape(*dims):
    return jax.ShapeDtypeStruct(dims, F32)


def split(x):
    high = x.astype(BF16)
    return high, (x - high.astype(F32)).astype(BF16)


def cosines(turns):
    turns = turns % L
    turns = jnp.where(turns > 8, L - turns, turns)
    near = jnp.where(turns > 4, 8 - turns, turns)
    value = jnp.zeros(turns.shape, F32)
    for step in range(4):
        value = jnp.where(near == step, math.cos(2.0 * math.pi * step / L) / L, value)
    return jnp.where(turns > 4, -value, value)


def phase_turns(lattice, site):
    return (lattice // L) * (site // L) + (lattice % L) * (site % L)


def table_body(lesser_ref, greater_ref, result_ref, *outs):
    rows = lax.broadcasted_iota(jnp.int32, (512, 512), 0)
    columns = lax.broadcasted_iota(jnp.int32, (512, 512), 1)
    forward = phase_turns(rows % 256, lesser_ref[...]) + 4 * ((columns // 16) % 2 - rows // 256)
    mirrored = phase_turns(rows % 256, greater_ref[...]) - 4 * ((columns // 4) % 2 - rows // 256)
    backward = phase_turns(columns % 256, result_ref[...]) + 4 * ((rows // 16) % 2 - columns // 256)
    for out, turns in zip(outs, (forward, mirrored, backward)):
        high, low = split(cosines(turns + L))
        out[:, 0:512] = high
        out[:, 512:1024] = low


def phase_tables(site_of):
    parts = jnp.broadcast_to(site_of.reshape(16, 1, 16), (16, 2, 16))
    columns = parts.reshape(512)
    quads = parts.reshape(16, 2, 4, 4).transpose(3, 0, 1, 2).reshape(1, 512)
    return pl.pallas_call(
        table_body,
        out_shape=(jax.ShapeDtypeStruct((512, 1024), BF16),) * 3,
        compiler_params=params(),
        cost_estimate=cost(),
    )(columns.reshape(1, 512), quads, columns.reshape(512, 1))


def times(table_ref, x):
    high, low = split(x)
    table_high, table_low = table_ref[:, 0:512], table_ref[:, 512:1024]
    product = jnp.dot(table_high, high, preferred_element_type=F32)
    product += jnp.dot(table_high, low, preferred_element_type=F32)
    return product + jnp.dot(table_low, high, preferred_element_type=F32)


def part(ref, m):
    return ref.at[:, :, m // 4, pl.ds(m % 4 * 8, 8), :]


def half(ref, m, h):
    return ref.at[m, :, :, :, pl.ds(128 * h, 128)]


def relay(loads, stores):
    for group in loads:
        for copy in group:
            copy.start()
    for group, after in zip(loads, stores):
        for copy in group:
            copy.wait()
        for copy in after:
            copy.start()
    for group in stores:
        for copy in group:
            copy.wait()


RELAY = [
    pltpu.VMEM((16, 2, 16, 8, 256), F32),
    pltpu.SemaphoreType.DMA((16,)),
    pltpu.SemaphoreType.DMA((16, 2)),
]


def shard_at(me, dz, dx, dc, way):
    x, z, c = me // 4, (me // 2) % 2, me % 2
    return ((x + way * dx + 4) % 4) * 4 + (z + dz) % 2 * 2 + (c + dc) % 2


def moved(values, dz, dx, dc):
    ways = [(m, (m // 4 + dx) % 4 * 4 + (m // 2 + dz) % 2 * 2 + (m + dc) % 2) for m in range(16)]
    return lax.ppermute(values, "mom", ways)


def pack_body(me_ref, after_ref, i_ref, *refs):
    near, far = refs[:2], refs[2:6]
    buffer, one, two = refs[6:]
    copy = pltpu.make_async_copy
    loads, stores = [], []
    for i, (dz, dx, dc) in enumerate(DISTANCES):
        source = part(i_ref, shard_at(me_ref[0], dz, dx, dc, 1))
        loads.append([copy(source, buffer.at[i], one.at[i])])
        stores.append(
            [
                copy(half(buffer, i, 0), near[dz].at[dx, dc], two.at[i, 0]),
                copy(half(buffer, i, 1), far[dx].at[dz, dc], two.at[i, 1]),
            ]
        )
    relay(loads, stores)


def pack(me, after, values):
    return pl.pallas_call(
        pack_body,
        in_specs=[SCALAR, HBM, HBM],
        out_specs=(HBM,) * 6,
        out_shape=(shape(4, 2, *BLOCK),) * 2 + (shape(2, 2, *BLOCK),) * 4,
        scratch_shapes=RELAY,
        compiler_params=params(),
        cost_estimate=cost(),
    )(me, after, values)


def gather(outs, arrays, ready):
    pairs = [(i, j, source) for i, blocks in enumerate(outs) for j, source in enumerate(blocks)]

    def body(*refs):
        made, (buffer, sems) = refs[-2 - len(outs) : -2], refs[-2:]
        copy = pltpu.make_async_copy
        relay(
            [
                [copy(refs[n].at[index], buffer.at[k], sems.at[0, k])]
                for k, (_, _, (n, index)) in enumerate(pairs)
            ],
            [
                [copy(buffer.at[k], made[i].at[j], sems.at[1, k])]
                for k, (i, j, _) in enumerate(pairs)
            ],
        )

    return pl.pallas_call(
        body,
        in_specs=[HBM] * (len(arrays) + len(ready)),
        out_specs=(HBM,) * len(outs),
        out_shape=tuple(shape(len(blocks), *BLOCK) for blocks in outs),
        scratch_shapes=[
            pltpu.VMEM((len(pairs), *BLOCK), F32),
            pltpu.SemaphoreType.DMA((2, len(pairs))),
        ],
        compiler_params=params(),
        cost_estimate=cost(),
    )(*arrays, *ready)


def exchange(sent, ready, between):
    near = [sent[0], moved(sent[1], 1, 0, 0)]
    far = [sent[2]] + [moved(sent[2 + dx], 0, dx, 0) for dx in range(1, 4)]
    over_z = [[(2 + dx, (1, dc)) for dx in range(4)] for dc in range(2)]
    over_x = [[(dz, (dx, dc)) for dz in range(2) for dc in range(2)] for dx in range(1, 4)]
    turned = gather([*over_z, *over_x], [*near, *far], ready)
    ways = [(1, 0, 0), (1, 0, 1), (0, 1, 0), (0, 2, 0), (0, 3, 0)]
    last = [moved(values, *way) for values, way in zip(turned, ways)]
    near += last[2:5]
    over_core = [
        (1 + dx, 2 * dz + 1) if dx else (dz, (0, 1)) for dz in range(2) for dx in range(4)
    ]
    disp = between(turned[0])
    (beside,) = gather([[(dx, (0, 1)) for dx in range(4)]], far, [disp])
    far = far + last[:2] + [moved(beside, 0, 0, 1)]
    (crossing,) = gather([over_core], near, [disp])
    near.append(moved(crossing, 0, 0, 1))
    return near, far + [crossing], disp


def arrived(refs, h, dz, dx, dc):
    if h == 0:
        if dc:
            return refs[5].at[4 * dz + dx]
        return refs[1 + dx].at[2 * dz] if dx else refs[dz].at[0, 0]
    if dz:
        return refs[4 + dc].at[dx]
    return refs[6].at[dx] if dc else refs[dx].at[0, 0]


def unpack_body(*refs):
    i_ref, (o_ref, buffer, one, two) = refs[0], refs[-4:]
    h = 6 - len(refs)
    copy = pltpu.make_async_copy
    relay(
        [[copy(i_ref.at[m], buffer.at[m], one.at[m])] for m in range(16)],
        [
            [copy(buffer.at[m], part(o_ref, m).at[:, :, :, pl.ds(128 * h, 128)], two.at[m])]
            for m in range(16)
        ],
    )


def unpack(values, *done):
    return pl.pallas_call(
        unpack_body,
        in_specs=[ANY] + [HBM] * len(done),
        out_specs=HBM,
        out_shape=shape(2, 16, 4, 32, 256),
        scratch_shapes=[
            pltpu.VMEM((16, *BLOCK), F32),
            pltpu.SemaphoreType.DMA((16,)),
            pltpu.SemaphoreType.DMA((16,)),
        ],
        input_output_aliases={1: 0} if done else {},
        compiler_params=params(),
        cost_estimate=cost(),
    )(values, *done)


def swap_rows(tiles):
    tiles = list(tiles)
    row = lax.broadcasted_iota(jnp.int32, tiles[0].shape, 1)
    for step in (4, 2, 1):
        keep = (row // step) % 2 == 0
        for i in range(8):
            if i // step % 2 == 0:
                a, b = tiles[i], tiles[i + step]
                tiles[i] = jnp.where(keep, a, pltpu.roll(b, step, 1))
                tiles[i + step] = jnp.where(keep, pltpu.roll(a, 8 - step, 1), b)
    return tiles


def pack_greater_body(i_ref, o_ref):
    for h in range(2):
        turned = []
        for c in range(2):
            for q in range(4):
                block = i_ref[c, 4 * q : 4 * q + 4, 0, :, 128 * h : 128 * h + 128]
                turned.append(block.reshape(128, 128).T.reshape(16, 8, 128))
        for t, tile in enumerate(swap_rows(turned)):
            for s in range(4):
                for g in range(4):
                    o_ref[0, g, 4 * h + s, t] = tile[4 * s + g]


def pack_greater(values):
    return pl.pallas_call(
        pack_greater_body,
        grid=(4,),
        in_specs=[
            pl.BlockSpec((2, 16, 1, 32, 256), lambda o: (0, 0, (o % 2) * 2 + o // 2, 0, 0))
        ],
        out_specs=pl.BlockSpec((1, 4, 8, 8, 8, 128), lambda o: (o, 0, 0, 0, 0, 0)),
        out_shape=shape(4, 4, 8, 8, 8, 128),
        compiler_params=params(),
        cost_estimate=cost(),
    )(values)


def swap_blocks(tiles):
    lane = lax.broadcasted_iota(jnp.int32, tiles[0].shape, 1)
    a, b, c, d = tiles
    low = lane < 64
    pairs = []
    for p, q in ((a, c), (b, d)):
        pairs.append(jnp.where(low, p, pltpu.roll(q, 64, 1)))
        pairs.append(jnp.where(low, pltpu.roll(p, 64, 1), q))
    e, f, g, h = pairs[0], pairs[2], pairs[1], pairs[3]
    even = (lane // 32) % 2 == 0
    return (
        jnp.where(even, e, pltpu.roll(f, 32, 1)),
        jnp.where(even, pltpu.roll(e, 96, 1), f),
        jnp.where(even, g, pltpu.roll(h, 32, 1)),
        jnp.where(even, pltpu.roll(g, 96, 1), h),
    )


ROWS = pl.BlockSpec((16, 1, 256, 128), lambda h, t: (0, h, 0, 0))
DISP = pl.BlockSpec((1, 1, 512, 256), lambda h, t: (h, t, 0, 0))
TABLE = pl.BlockSpec((512, 1024), lambda h, t: (0, 0))


def greater_body(after_ref, x_ref, table_ref, o_ref):
    pairs = []
    for i in range(2):
        tiles = [x_ref[:, s, i].reshape(128, 128) for s in range(4)]
        pairs.append(jnp.concatenate(swap_blocks(tiles), 0))
    o_ref[0, 0] = times(table_ref, jnp.concatenate(pairs, 1))


def greater_transform(after, rows, table):
    return pl.pallas_call(
        greater_body,
        grid=(2, 4),
        in_specs=[HBM, pl.BlockSpec((16, 4, 2, 8, 128), lambda h, t: (0, h, t, 0, 0)), TABLE],
        out_specs=DISP,
        out_shape=shape(2, 4, 512, 256),
        compiler_params=params(),
        cost_estimate=cost(),
    )(after, rows, table)


def bubble(lesser, greater):
    lr, li = lesser[0:256], lesser[256:512]
    gr, gi = greater[0:256], greater[256:512]
    return jnp.concatenate([lr * gi + li * gr, li * gi - lr * gr], 0)


def bubble_body(h, me_ref, g_ref, forward_ref, backward_ref, *refs):
    held, (o_ref, rows_ref, result_ref, sems) = refs[:-4], refs[-4:]
    step = pl.program_id(0)

    @pl.when(step == 0)
    def _():
        copies = [
            pltpu.make_async_copy(
                arrived(held, h, dz, dx, dc),
                rows_ref.at[shard_at(me_ref[0], dz, dx, dc, -1)],
                sems.at[i],
            )
            for i, (dz, dx, dc) in enumerate(DISTANCES)
        ]
        for copy in copies:
            copy.start()
        for copy in copies:
            copy.wait()

    rows = rows_ref.reshape(4096, 128)
    x = jnp.concatenate([rows[pl.ds(2 * step + i, 512, stride=8), :] for i in range(2)], 1)
    result = times(backward_ref, bubble(times(forward_ref, x), g_ref[0, 0]))
    for i in range(2):
        result_ref[2 * step + i] = result[:, 128 * i : 128 * i + 128]

    @pl.when(step == 3)
    def _():
        def shard(m, carry):
            row = pl.multiple_of(32 * m, 32)
            tiles = [result_ref[t, pl.ds(row, 32), :].reshape(4, 8, 128) for t in range(8)]
            o_ref[m] = jnp.stack(swap_rows(tiles), 1).reshape(256, 128)
            return carry

        lax.fori_loop(0, 16, shard, 0)


def bubble_transform(h, me, held, greater_disp, forward, backward):
    table = pl.BlockSpec((512, 1024), lambda t: (0, 0))
    return pl.pallas_call(
        functools.partial(bubble_body, h),
        grid=(4,),
        in_specs=[SCALAR, pl.BlockSpec((1, 1, 512, 256), lambda t: (h, t, 0, 0)), table, table]
        + [HBM] * len(held),
        out_specs=pl.BlockSpec((16, 256, 128), lambda t: (0, 0, 0)),
        out_shape=shape(16, 256, 128),
        scratch_shapes=[
            pltpu.VMEM((16, *BLOCK), F32),
            pltpu.VMEM((8, 512, 128), F32),
            pltpu.SemaphoreType.DMA((16,)),
        ],
        compiler_params=params(),
        cost_estimate=cost(),
    )(me, greater_disp, forward, backward, *held)


def local(lesser, greater, site_of):
    merged = (2, 16, 4, 32, 256)
    me = lax.axis_index("mom").reshape(1)
    greater_out = pack_greater(greater.reshape(merged))
    greater_rows = lax.all_to_all(
        greater_out.reshape(128, 64, 128), ("mom", "tm"), 0, 0, tiled=True
    ).reshape(16, 8, 8, 8, 128)
    sent = pack(me, greater_out, lesser.reshape(merged))
    forward, mirrored, backward = phase_tables(site_of)
    near, far, disp = exchange(
        sent, (forward,), lambda turned: greater_transform(turned, greater_rows, mirrored)
    )
    far = bubble_transform(1, me, far, disp, forward, backward)
    far = lax.all_to_all(far, "mom", 0, 0, tiled=True).reshape(16, *BLOCK)
    near = bubble_transform(0, me, near, disp, forward, backward)
    near = lax.all_to_all(near, "mom", 0, 0, tiled=True).reshape(16, *BLOCK)
    return unpack(near, unpack(far)).reshape(lesser.shape)


def solution(mesh):
    in_specs = (P(None, "mom", None, None, "tm", None), P(None, "mom", None, None, "tm", None), P())
    out_specs = P(None, "mom", None, None, "tm", None)
    return jax.shard_map(local, mesh=mesh, in_specs=in_specs, out_specs=out_specs, check_vma=False)
```

```python
import functools
import math

import jax
import jax.numpy as jnp
from jax import lax
from jax.experimental import pallas as pl
from jax.experimental.pallas import tpu as pltpu
from jax.sharding import PartitionSpec as P

L = 16
VMEM = 56 * 1024 * 1024
F32 = jnp.float32
BF16 = jnp.bfloat16
BLOCK = (2, 16, 8, 128)
ANY = pl.BlockSpec(memory_space=pl.ANY)
HBM = pl.BlockSpec(memory_space=pltpu.HBM)
SCALAR = pl.BlockSpec(memory_space=pltpu.SMEM)
DISTANCES = [(dz, dx, dc) for dz in range(2) for dx in range(4) for dc in range(2)]


def params():
    return pltpu.CompilerParams(vmem_limit_bytes=VMEM)


def cost():
    return pl.CostEstimate(flops=1, bytes_accessed=1, transcendentals=0)


def shape(*dims):
    return jax.ShapeDtypeStruct(dims, F32)


def split(x):
    high = x.astype(BF16)
    return high, (x - high.astype(F32)).astype(BF16)


def cosines(turns):
    turns = turns % L
    turns = jnp.where(turns > 8, L - turns, turns)
    near = jnp.where(turns > 4, 8 - turns, turns)
    value = jnp.zeros(turns.shape, F32)
    for step in range(4):
        value = jnp.where(near == step, math.cos(2.0 * math.pi * step / L) / L, value)
    return jnp.where(turns > 4, -value, value)


def phase_turns(lattice, site):
    return (lattice // L) * (site // L) + (lattice % L) * (site % L)


def table_body(lesser_ref, greater_ref, result_ref, *outs):
    rows = lax.broadcasted_iota(jnp.int32, (512, 512), 0)
    columns = lax.broadcasted_iota(jnp.int32, (512, 512), 1)
    forward = phase_turns(rows % 256, lesser_ref[...]) + 4 * ((columns // 16) % 2 - rows // 256)
    mirrored = phase_turns(rows % 256, greater_ref[...]) - 4 * ((columns // 4) % 2 - rows // 256)
    backward = phase_turns(columns % 256, result_ref[...]) + 4 * ((rows // 16) % 2 - columns // 256)
    for out, turns in zip(outs, (forward, mirrored, backward)):
        high, low = split(cosines(turns + L))
        out[:, 0:512] = high
        out[:, 512:1024] = low


def phase_tables(site_of):
    parts = jnp.broadcast_to(site_of.reshape(16, 1, 16), (16, 2, 16))
    columns = parts.reshape(512)
    quads = parts.reshape(16, 2, 4, 4).transpose(3, 0, 1, 2).reshape(1, 512)
    return pl.pallas_call(
        table_body,
        out_shape=(jax.ShapeDtypeStruct((512, 1024), BF16),) * 3,
        compiler_params=params(),
        cost_estimate=cost(),
    )(columns.reshape(1, 512), quads, columns.reshape(512, 1))


def times(table_ref, x):
    high, low = split(x)
    table_high, table_low = table_ref[:, 0:512], table_ref[:, 512:1024]
    tables = jnp.concatenate([table_high, table_high, table_low], 1)
    return jnp.dot(tables, jnp.concatenate([high, low, high], 0), preferred_element_type=F32)


def part(ref, m):
    return ref.at[:, :, m // 4, pl.ds(m % 4 * 8, 8), :]


def half(ref, m, h):
    return ref.at[m, :, :, :, pl.ds(128 * h, 128)]


def relay(loads, stores):
    for group in loads:
        for copy in group:
            copy.start()
    for group, after in zip(loads, stores):
        for copy in group:
            copy.wait()
        for copy in after:
            copy.start()
    for group in stores:
        for copy in group:
            copy.wait()


RELAY = [
    pltpu.VMEM((16, 2, 16, 8, 256), F32),
    pltpu.SemaphoreType.DMA((16,)),
    pltpu.SemaphoreType.DMA((16, 2)),
]


def shard_at(me, dz, dx, dc, way):
    x, z, c = me // 4, (me // 2) % 2, me % 2
    return ((x + way * dx + 4) % 4) * 4 + (z + dz) % 2 * 2 + (c + dc) % 2


def moved(values, dz, dx, dc):
    ways = [(m, (m // 4 + dx) % 4 * 4 + (m // 2 + dz) % 2 * 2 + (m + dc) % 2) for m in range(16)]
    return lax.ppermute(values, "mom", ways)


def pack_body(me_ref, after_ref, i_ref, *refs):
    near, far = refs[:2], refs[2:6]
    buffer, one, two = refs[6:]
    copy = pltpu.make_async_copy
    loads, stores = [], []
    for i, (dz, dx, dc) in enumerate(DISTANCES):
        source = part(i_ref, shard_at(me_ref[0], dz, dx, dc, 1))
        loads.append([copy(source, buffer.at[i], one.at[i])])
        stores.append(
            [
                copy(half(buffer, i, 0), near[dz].at[dx, dc], two.at[i, 0]),
                copy(half(buffer, i, 1), far[dx].at[dz, dc], two.at[i, 1]),
            ]
        )
    relay(loads, stores)


def pack(me, after, values):
    return pl.pallas_call(
        pack_body,
        in_specs=[SCALAR, HBM, HBM],
        out_specs=(HBM,) * 6,
        out_shape=(shape(4, 2, *BLOCK),) * 2 + (shape(2, 2, *BLOCK),) * 4,
        scratch_shapes=RELAY,
        compiler_params=params(),
        cost_estimate=cost(),
    )(me, after, values)


def gather(outs, arrays, ready):
    pairs = [(i, j, source) for i, blocks in enumerate(outs) for j, source in enumerate(blocks)]

    def body(*refs):
        made, (buffer, sems) = refs[-2 - len(outs) : -2], refs[-2:]
        copy = pltpu.make_async_copy
        relay(
            [
                [copy(refs[n].at[index], buffer.at[k], sems.at[0, k])]
                for k, (_, _, (n, index)) in enumerate(pairs)
            ],
            [
                [copy(buffer.at[k], made[i].at[j], sems.at[1, k])]
                for k, (i, j, _) in enumerate(pairs)
            ],
        )

    return pl.pallas_call(
        body,
        in_specs=[ANY] * len(arrays) + [HBM] * len(ready),
        out_specs=(HBM,) * len(outs),
        out_shape=tuple(shape(len(blocks), *BLOCK) for blocks in outs),
        scratch_shapes=[
            pltpu.VMEM((len(pairs), *BLOCK), F32),
            pltpu.SemaphoreType.DMA((2, len(pairs))),
        ],
        compiler_params=params(),
        cost_estimate=cost(),
    )(*arrays, *ready)


def exchange(sent, ready, between):
    near = [sent[0], moved(sent[1], 1, 0, 0)]
    far = [sent[2]] + [moved(sent[2 + dx], 0, dx, 0) for dx in range(1, 4)]
    over_z = [[(2 + dx, (1, dc)) for dx in range(4)] for dc in range(2)]
    over_x = [[(dz, (dx, dc)) for dz in range(2) for dc in range(2)] for dx in range(1, 4)]
    turned = gather([*over_z, *over_x], [*near, *far], ready)
    ways = [(1, 0, 0), (1, 0, 1), (0, 1, 0), (0, 2, 0), (0, 3, 0)]
    last = [moved(values, *way) for values, way in zip(turned, ways)]
    near += last[2:5]
    over_core = [
        (1 + dx, 2 * dz + 1) if dx else (dz, (0, 1)) for dz in range(2) for dx in range(4)
    ]
    disp = between(turned[0])
    (beside,) = gather([[(dx, (0, 1)) for dx in range(4)]], far, [disp])
    far = far + last[:2] + [moved(beside, 0, 0, 1)]
    (crossing,) = gather([over_core], near, [disp])
    near.append(moved(crossing, 0, 0, 1))
    return near, far, crossing, disp


def arrived(refs, h, dz, dx, dc):
    if h == 0:
        if dc:
            return refs[5].at[4 * dz + dx]
        return refs[1 + dx].at[2 * dz] if dx else refs[dz].at[0, 0]
    if dz:
        return refs[4 + dc].at[dx]
    return refs[6].at[dx] if dc else refs[dx].at[0, 0]


def unpack_body(*refs):
    i_ref, (o_ref, buffer, one, two) = refs[0], refs[-4:]
    h = 6 - len(refs)
    copy = pltpu.make_async_copy
    relay(
        [[copy(i_ref.at[m], buffer.at[m], one.at[m])] for m in range(16)],
        [
            [copy(buffer.at[m], part(o_ref, m).at[:, :, :, pl.ds(128 * h, 128)], two.at[m])]
            for m in range(16)
        ],
    )


def unpack(values, *done):
    return pl.pallas_call(
        unpack_body,
        in_specs=[ANY] + [HBM] * len(done),
        out_specs=HBM,
        out_shape=shape(2, 16, 4, 32, 256),
        scratch_shapes=[
            pltpu.VMEM((16, *BLOCK), F32),
            pltpu.SemaphoreType.DMA((16,)),
            pltpu.SemaphoreType.DMA((16,)),
        ],
        input_output_aliases={1: 0} if done else {},
        compiler_params=params(),
        cost_estimate=cost(),
    )(values, *done)


def swap_rows(tiles):
    tiles = list(tiles)
    row = lax.broadcasted_iota(jnp.int32, tiles[0].shape, 1)
    for step in (4, 2, 1):
        keep = (row // step) % 2 == 0
        for i in range(8):
            if i // step % 2 == 0:
                a, b = tiles[i], tiles[i + step]
                tiles[i] = jnp.where(keep, a, pltpu.roll(b, step, 1))
                tiles[i + step] = jnp.where(keep, pltpu.roll(a, 8 - step, 1), b)
    return tiles


def pack_greater_body(i_ref, o_ref):
    for h in range(2):
        turned = []
        for c in range(2):
            for q in range(4):
                block = i_ref[c, 4 * q : 4 * q + 4, 0, :, 128 * h : 128 * h + 128]
                turned.append(block.reshape(128, 128).T.reshape(16, 8, 128))
        for t, tile in enumerate(swap_rows(turned)):
            for s in range(4):
                for g in range(4):
                    o_ref[0, g, 4 * h + s, t] = tile[4 * s + g]


def pack_greater(values):
    return pl.pallas_call(
        pack_greater_body,
        grid=(4,),
        in_specs=[
            pl.BlockSpec((2, 16, 1, 32, 256), lambda o: (0, 0, (o % 2) * 2 + o // 2, 0, 0))
        ],
        out_specs=pl.BlockSpec((1, 4, 8, 8, 8, 128), lambda o: (o, 0, 0, 0, 0, 0)),
        out_shape=shape(4, 4, 8, 8, 8, 128),
        compiler_params=params(),
        cost_estimate=cost(),
    )(values)


def swap_blocks(tiles):
    lane = lax.broadcasted_iota(jnp.int32, tiles[0].shape, 1)
    a, b, c, d = tiles
    low = lane < 64
    pairs = []
    for p, q in ((a, c), (b, d)):
        pairs.append(jnp.where(low, p, pltpu.roll(q, 64, 1)))
        pairs.append(jnp.where(low, pltpu.roll(p, 64, 1), q))
    e, f, g, h = pairs[0], pairs[2], pairs[1], pairs[3]
    even = (lane // 32) % 2 == 0
    return (
        jnp.where(even, e, pltpu.roll(f, 32, 1)),
        jnp.where(even, pltpu.roll(e, 96, 1), f),
        jnp.where(even, g, pltpu.roll(h, 32, 1)),
        jnp.where(even, pltpu.roll(g, 96, 1), h),
    )


WIDE = 4


def greater_body(after_ref, x_ref, table_ref, o_ref):
    parts = []
    for i in range(WIDE):
        tiles = [x_ref[:, s, i].reshape(128, 128) for s in range(4)]
        parts.append(jnp.concatenate(swap_blocks(tiles), 0))
    o_ref[0, 0] = times(table_ref, jnp.concatenate(parts, 1))


def greater_transform(after, rows, table):
    steps = 8 // WIDE
    return pl.pallas_call(
        greater_body,
        grid=(2, steps),
        in_specs=[
            HBM,
            pl.BlockSpec((16, 4, WIDE, 8, 128), lambda h, t: (0, h, t, 0, 0)),
            pl.BlockSpec((512, 1024), lambda h, t: (0, 0)),
        ],
        out_specs=pl.BlockSpec((1, 1, 512, 128 * WIDE), lambda h, t: (h, t, 0, 0)),
        out_shape=shape(2, steps, 512, 128 * WIDE),
        compiler_params=params(),
        cost_estimate=cost(),
    )(after, rows, table)


def bubble(lesser, greater):
    lr, li = lesser[0:256], lesser[256:512]
    gr, gi = greater[0:256], greater[256:512]
    return jnp.concatenate([lr * gi + li * gr, li * gi - lr * gr], 0)


def bubble_body(h, me_ref, g_ref, forward_hbm, backward_hbm, *refs):
    held, out_ref, scratch = refs[:-9], refs[-9], refs[-8:]
    rows_ref, turned_ref, result_ref, o_ref, forward_ref, backward_ref, sems, others = scratch
    step = pl.program_id(0)

    @pl.when(step == 0)
    def _():
        tables = [
            pltpu.make_async_copy(forward_hbm, forward_ref, others.at[0]),
            pltpu.make_async_copy(backward_hbm, backward_ref, others.at[1]),
        ]
        shards = [shard_at(me_ref[0], dz, dx, dc, -1) for dz, dx, dc in DISTANCES]
        copies = [
            pltpu.make_async_copy(arrived(held, h, *way), rows_ref.at[i], sems.at[i])
            for i, way in enumerate(DISTANCES)
        ]
        for copy in copies + tables:
            copy.start()
        for i, (copy, shard) in enumerate(zip(copies, shards)):
            copy.wait()
            tiles = rows_ref[i].reshape(4, 8, 8, 128)
            row = pl.multiple_of(32 * shard, 32)
            for t, tile in enumerate(swap_rows([tiles[:, j] for j in range(8)])):
                turned_ref[t, pl.ds(row, 32), :] = tile.reshape(32, 128)
        for copy in tables:
            copy.wait()

    x = jnp.concatenate([turned_ref[WIDE * step + i] for i in range(WIDE)], 1)
    result = times(backward_ref, bubble(times(forward_ref, x), g_ref[0, 0]))
    for i in range(WIDE):
        result_ref[WIDE * step + i] = result[:, 128 * i : 128 * i + 128]

    @pl.when(step == 8 // WIDE - 1)
    def _():
        copies = [pltpu.make_async_copy(o_ref.at[m], out_ref.at[m], sems.at[m]) for m in range(16)]
        for m in range(16):
            tiles = [
                result_ref[t, 32 * m : 32 * m + 32, :].reshape(4, 8, 128) for t in range(8)
            ]
            o_ref[m] = jnp.stack(swap_rows(tiles), 1).reshape(256, 128)
            copies[m].start()
        for copy in copies:
            copy.wait()


def bubble_transform(h, me, held, greater_disp, forward, backward, after=()):
    return pl.pallas_call(
        functools.partial(bubble_body, h),
        grid=(8 // WIDE,),
        in_specs=[SCALAR, pl.BlockSpec((1, 1, 512, 128 * WIDE), lambda t: (h, t, 0, 0)), HBM, HBM]
        + [ANY] * len(held)
        + [HBM] * len(after),
        out_specs=HBM,
        out_shape=shape(16, 256, 128),
        scratch_shapes=[
            pltpu.VMEM((16, *BLOCK), F32),
            pltpu.VMEM((8, 512, 128), F32),
            pltpu.VMEM((8, 512, 128), F32),
            pltpu.VMEM((16, 256, 128), F32),
            pltpu.VMEM((512, 1024), BF16),
            pltpu.VMEM((512, 1024), BF16),
            pltpu.SemaphoreType.DMA((16,)),
            pltpu.SemaphoreType.DMA((2,)),
        ],
        compiler_params=params(),
        cost_estimate=cost(),
    )(me, greater_disp, forward, backward, *held, *after)


def local(lesser, greater, site_of):
    merged = (2, 16, 4, 32, 256)
    me = lax.axis_index("mom").reshape(1)
    greater_out = pack_greater(greater.reshape(merged))
    greater_rows = lax.all_to_all(
        greater_out.reshape(128, 64, 128), ("mom", "tm"), 0, 0, tiled=True
    ).reshape(16, 8, 8, 8, 128)
    sent = pack(me, greater_out, lesser.reshape(merged))
    forward, mirrored, backward = phase_tables(site_of)
    near, far, crossing, disp = exchange(
        sent, (forward,), lambda turned: greater_transform(turned, greater_rows, mirrored)
    )
    far = bubble_transform(1, me, far, disp, forward, backward, (crossing,))
    far = lax.all_to_all(far, "mom", 0, 0, tiled=True).reshape(16, *BLOCK)
    near = bubble_transform(0, me, near, disp, forward, backward)
    near = lax.all_to_all(near, "mom", 0, 0, tiled=True).reshape(16, *BLOCK)
    return unpack(near, unpack(far)).reshape(lesser.shape)


def solution(mesh):
    in_specs = (P(None, "mom", None, None, "tm", None), P(None, "mom", None, None, "tm", None), P())
    out_specs = P(None, "mom", None, None, "tm", None)
    return jax.shard_map(local, mesh=mesh, in_specs=in_specs, out_specs=out_specs, check_vma=False)
```

```python
import functools
import math

import jax
import jax.numpy as jnp
from jax import lax
from jax.experimental import pallas as pl
from jax.experimental.pallas import tpu as pltpu
from jax.sharding import PartitionSpec as P

L = 16
VMEM = 63 * 1024 * 1024
F32 = jnp.float32
BF16 = jnp.bfloat16
BLOCK = (2, 16, 8, 128)
ANY = pl.BlockSpec(memory_space=pl.ANY)
HBM = pl.BlockSpec(memory_space=pltpu.HBM)
SCALAR = pl.BlockSpec(memory_space=pltpu.SMEM)
DISTANCES = [(dz, dx, dc) for dz in range(2) for dx in range(4) for dc in range(2)]


def params():
    return pltpu.CompilerParams(vmem_limit_bytes=VMEM)


def cost():
    return pl.CostEstimate(flops=1, bytes_accessed=1, transcendentals=0)


def shape(*dims):
    return jax.ShapeDtypeStruct(dims, F32)


def split(x):
    high = x.astype(BF16)
    return high, (x - high.astype(F32)).astype(BF16)


def cosines(turns):
    turns = turns % L
    turns = jnp.where(turns > 8, L - turns, turns)
    near = jnp.where(turns > 4, 8 - turns, turns)
    value = jnp.zeros(turns.shape, F32)
    for step in range(4):
        value = jnp.where(near == step, math.cos(2.0 * math.pi * step / L) / L, value)
    return jnp.where(turns > 4, -value, value)


def phase_turns(lattice, site):
    return (lattice // L) * (site // L) + (lattice % L) * (site % L)


def table_body(lesser_ref, greater_ref, result_ref, *outs):
    rows = lax.broadcasted_iota(jnp.int32, (512, 512), 0)
    columns = lax.broadcasted_iota(jnp.int32, (512, 512), 1)
    forward = phase_turns(rows % 256, lesser_ref[...]) + 4 * ((columns // 16) % 2 - rows // 256)
    mirrored = phase_turns(rows % 256, greater_ref[...]) - 4 * ((columns // 4) % 2 - rows // 256)
    backward = phase_turns(columns % 256, result_ref[...]) + 4 * ((rows // 16) % 2 - columns // 256)
    for out, turns in zip(outs, (forward, mirrored, backward)):
        high, low = split(cosines(turns + L))
        out[:, 0:512] = high
        out[:, 512:1024] = low


def phase_tables(site_of):
    parts = jnp.broadcast_to(site_of.reshape(16, 1, 16), (16, 2, 16))
    columns = parts.reshape(512)
    quads = parts.reshape(16, 2, 4, 4).transpose(3, 0, 1, 2).reshape(1, 512)
    return pl.pallas_call(
        table_body,
        out_shape=(jax.ShapeDtypeStruct((512, 1024), BF16),) * 3,
        compiler_params=params(),
        cost_estimate=cost(),
    )(columns.reshape(1, 512), quads, columns.reshape(512, 1))


def times(table_ref, x):
    high, low = split(x)
    table_high, table_low = table_ref[:, 0:512], table_ref[:, 512:1024]
    tables = jnp.concatenate([table_high, table_high, table_low], 1)
    return jnp.dot(tables, jnp.concatenate([high, low, high], 0), preferred_element_type=F32)


def part(ref, m):
    return ref.at[:, :, m // 4, pl.ds(m % 4 * 8, 8), :]


def half(ref, m, h):
    return ref.at[m, :, :, :, pl.ds(128 * h, 128)]


def relay(loads, stores):
    for group in loads:
        for copy in group:
            copy.start()
    for group, after in zip(loads, stores):
        for copy in group:
            copy.wait()
        for copy in after:
            copy.start()
    for group in stores:
        for copy in group:
            copy.wait()


RELAY = [
    pltpu.VMEM((16, 2, 16, 8, 256), F32),
    pltpu.SemaphoreType.DMA((16,)),
    pltpu.SemaphoreType.DMA((16, 2)),
]


def shard_at(me, dz, dx, dc, way):
    x, z, c = me // 4, (me // 2) % 2, me % 2
    return ((x + way * dx + 4) % 4) * 4 + (z + dz) % 2 * 2 + (c + dc) % 2


def moved(values, dz, dx, dc):
    ways = [(m, (m // 4 + dx) % 4 * 4 + (m // 2 + dz) % 2 * 2 + (m + dc) % 2) for m in range(16)]
    return lax.ppermute(values, "mom", ways)


def pack_body(me_ref, after_ref, i_ref, *refs):
    near, far = refs[:2], refs[2:6]
    buffer, one, two = refs[6:]
    copy = pltpu.make_async_copy
    loads, stores = [], []
    for i, (dz, dx, dc) in enumerate(DISTANCES):
        source = part(i_ref, shard_at(me_ref[0], dz, dx, dc, 1))
        loads.append([copy(source, buffer.at[i], one.at[i])])
        stores.append(
            [
                copy(half(buffer, i, 0), near[dz].at[dx, dc], two.at[i, 0]),
                copy(half(buffer, i, 1), far[dx].at[dz, dc], two.at[i, 1]),
            ]
        )
    relay(loads, stores)


def pack(me, after, values):
    return pl.pallas_call(
        pack_body,
        in_specs=[SCALAR, HBM, HBM],
        out_specs=(HBM,) * 6,
        out_shape=(shape(4, 2, *BLOCK),) * 2 + (shape(2, 2, *BLOCK),) * 4,
        scratch_shapes=RELAY,
        compiler_params=params(),
        cost_estimate=cost(),
    )(me, after, values)


def gather(outs, arrays, ready):
    pairs = [(i, j, source) for i, blocks in enumerate(outs) for j, source in enumerate(blocks)]

    def body(*refs):
        made, (buffer, sems) = refs[-2 - len(outs) : -2], refs[-2:]
        copy = pltpu.make_async_copy
        relay(
            [
                [copy(refs[n].at[index], buffer.at[k], sems.at[0, k])]
                for k, (_, _, (n, index)) in enumerate(pairs)
            ],
            [
                [copy(buffer.at[k], made[i].at[j], sems.at[1, k])]
                for k, (i, j, _) in enumerate(pairs)
            ],
        )

    return pl.pallas_call(
        body,
        in_specs=[ANY] * len(arrays) + [HBM] * len(ready),
        out_specs=(HBM,) * len(outs),
        out_shape=tuple(shape(len(blocks), *BLOCK) for blocks in outs),
        scratch_shapes=[
            pltpu.VMEM((len(pairs), *BLOCK), F32),
            pltpu.SemaphoreType.DMA((2, len(pairs))),
        ],
        compiler_params=params(),
        cost_estimate=cost(),
    )(*arrays, *ready)


def exchange(sent, ready, between):
    near = [sent[0], moved(sent[1], 1, 0, 0)]
    far = [sent[2]] + [moved(sent[2 + dx], 0, dx, 0) for dx in range(1, 4)]
    over_z = [[(2 + dx, (1, dc)) for dx in range(4)] for dc in range(2)]
    over_x = [[(dz, (dx, dc)) for dz in range(2) for dc in range(2)] for dx in range(1, 4)]
    turned = gather([*over_z, *over_x], [*near, *far], ready)
    ways = [(1, 0, 0), (1, 0, 1), (0, 1, 0), (0, 2, 0), (0, 3, 0)]
    last = [moved(values, *way) for values, way in zip(turned, ways)]
    near += last[2:5]
    over_core = [
        (1 + dx, 2 * dz + 1) if dx else (dz, (0, 1)) for dz in range(2) for dx in range(4)
    ]
    disp = between(turned[0])
    (beside,) = gather([[(dx, (0, 1)) for dx in range(4)]], far, [disp])
    far = far + last[:2] + [moved(beside, 0, 0, 1)]
    (crossing,) = gather([over_core], near, [disp])
    near.append(moved(crossing, 0, 0, 1))
    return near, far, crossing, disp


def arrived(refs, h, dz, dx, dc):
    if h == 0:
        if dc:
            return refs[5].at[4 * dz + dx]
        return refs[1 + dx].at[2 * dz] if dx else refs[dz].at[0, 0]
    if dz:
        return refs[4 + dc].at[dx]
    return refs[6].at[dx] if dc else refs[dx].at[0, 0]


def unpack_body(*refs):
    i_ref, (o_ref, buffer, one, two) = refs[0], refs[-4:]
    h = 6 - len(refs)
    copy = pltpu.make_async_copy
    relay(
        [[copy(i_ref.at[m], buffer.at[m], one.at[m])] for m in range(16)],
        [
            [copy(buffer.at[m], part(o_ref, m).at[:, :, :, pl.ds(128 * h, 128)], two.at[m])]
            for m in range(16)
        ],
    )


def unpack(values, *done):
    return pl.pallas_call(
        unpack_body,
        in_specs=[ANY] + [HBM] * len(done),
        out_specs=HBM,
        out_shape=shape(2, 16, 4, 32, 256),
        scratch_shapes=[
            pltpu.VMEM((16, *BLOCK), F32),
            pltpu.SemaphoreType.DMA((16,)),
            pltpu.SemaphoreType.DMA((16,)),
        ],
        input_output_aliases={1: 0} if done else {},
        compiler_params=params(),
        cost_estimate=cost(),
    )(values, *done)


def swap_rows(tiles):
    tiles = list(tiles)
    row = lax.broadcasted_iota(jnp.int32, tiles[0].shape, 1)
    for step in (4, 2, 1):
        keep = (row // step) % 2 == 0
        for i in range(8):
            if i // step % 2 == 0:
                a, b = tiles[i], tiles[i + step]
                tiles[i] = jnp.where(keep, a, pltpu.roll(b, step, 1))
                tiles[i + step] = jnp.where(keep, pltpu.roll(a, 8 - step, 1), b)
    return tiles


def pack_greater_body(i_ref, o_ref):
    for h in range(2):
        turned = []
        for c in range(2):
            for q in range(4):
                block = i_ref[c, 4 * q : 4 * q + 4, 0, :, 128 * h : 128 * h + 128]
                turned.append(block.reshape(128, 128).T.reshape(16, 8, 128))
        for t, tile in enumerate(swap_rows(turned)):
            for s in range(4):
                for g in range(4):
                    o_ref[0, g, 4 * h + s, t] = tile[4 * s + g]


def pack_greater(values):
    return pl.pallas_call(
        pack_greater_body,
        grid=(4,),
        in_specs=[
            pl.BlockSpec((2, 16, 1, 32, 256), lambda o: (0, 0, (o % 2) * 2 + o // 2, 0, 0))
        ],
        out_specs=pl.BlockSpec((1, 4, 8, 8, 8, 128), lambda o: (o, 0, 0, 0, 0, 0)),
        out_shape=shape(4, 4, 8, 8, 8, 128),
        compiler_params=params(),
        cost_estimate=cost(),
    )(values)


def swap_blocks(tiles):
    lane = lax.broadcasted_iota(jnp.int32, tiles[0].shape, 1)
    a, b, c, d = tiles
    low = lane < 64
    pairs = []
    for p, q in ((a, c), (b, d)):
        pairs.append(jnp.where(low, p, pltpu.roll(q, 64, 1)))
        pairs.append(jnp.where(low, pltpu.roll(p, 64, 1), q))
    e, f, g, h = pairs[0], pairs[2], pairs[1], pairs[3]
    even = (lane // 32) % 2 == 0
    return (
        jnp.where(even, e, pltpu.roll(f, 32, 1)),
        jnp.where(even, pltpu.roll(e, 96, 1), f),
        jnp.where(even, g, pltpu.roll(h, 32, 1)),
        jnp.where(even, pltpu.roll(g, 96, 1), h),
    )


WIDE = 4


def greater_body(after_ref, x_ref, table_ref, o_ref):
    parts = []
    for i in range(WIDE):
        tiles = [x_ref[:, s, i].reshape(128, 128) for s in range(4)]
        parts.append(jnp.concatenate(swap_blocks(tiles), 0))
    o_ref[0, 0] = times(table_ref, jnp.concatenate(parts, 1))


def greater_transform(after, rows, table):
    steps = 8 // WIDE
    return pl.pallas_call(
        greater_body,
        grid=(2, steps),
        in_specs=[
            HBM,
            pl.BlockSpec((16, 4, WIDE, 8, 128), lambda h, t: (0, h, t, 0, 0)),
            pl.BlockSpec((512, 1024), lambda h, t: (0, 0)),
        ],
        out_specs=pl.BlockSpec((1, 1, 512, 128 * WIDE), lambda h, t: (h, t, 0, 0)),
        out_shape=shape(2, steps, 512, 128 * WIDE),
        compiler_params=params(),
        cost_estimate=cost(),
    )(after, rows, table)


def bubble(lesser, greater):
    lr, li = lesser[0:256], lesser[256:512]
    gr, gi = greater[0:256], greater[256:512]
    return jnp.concatenate([lr * gi + li * gr, li * gi - lr * gr], 0)


def bubble_body(h, me_ref, g_ref, forward_hbm, backward_hbm, *refs):
    held, out_ref, scratch = refs[:-9], refs[-9], refs[-8:]
    rows_ref, turned_ref, result_ref, o_ref, forward_ref, backward_ref, sems, others = scratch
    step = pl.program_id(0)

    @pl.when(step == 0)
    def _():
        tables = [
            pltpu.make_async_copy(forward_hbm, forward_ref, others.at[0]),
            pltpu.make_async_copy(backward_hbm, backward_ref, others.at[1]),
        ]
        shards = [shard_at(me_ref[0], dz, dx, dc, -1) for dz, dx, dc in DISTANCES]
        copies = [
            pltpu.make_async_copy(arrived(held, h, *way), rows_ref.at[i], sems.at[i])
            for i, way in enumerate(DISTANCES)
        ]
        for copy in copies + tables:
            copy.start()
        for i, (copy, shard) in enumerate(zip(copies, shards)):
            copy.wait()
            tiles = rows_ref[i].reshape(4, 8, 8, 128)
            row = pl.multiple_of(32 * shard, 32)
            for t, tile in enumerate(swap_rows([tiles[:, j] for j in range(8)])):
                turned_ref[t, pl.ds(row, 32), :] = tile.reshape(32, 128)
        for copy in tables:
            copy.wait()

    x = jnp.concatenate([turned_ref[WIDE * step + i] for i in range(WIDE)], 1)
    result = times(backward_ref, bubble(times(forward_ref, x), g_ref[0, 0]))
    for i in range(WIDE):
        result_ref[WIDE * step + i] = result[:, 128 * i : 128 * i + 128]

    @pl.when(step == 8 // WIDE - 1)
    def _():
        copies = [pltpu.make_async_copy(o_ref.at[m], out_ref.at[m], sems.at[m]) for m in range(16)]
        for m in range(16):
            tiles = [
                result_ref[t, 32 * m : 32 * m + 32, :].reshape(4, 8, 128) for t in range(8)
            ]
            o_ref[m] = jnp.stack(swap_rows(tiles), 1).reshape(256, 128)
            copies[m].start()
        for copy in copies:
            copy.wait()


def bubble_transform(h, me, held, greater_disp, forward, backward, after=()):
    return pl.pallas_call(
        functools.partial(bubble_body, h),
        grid=(8 // WIDE,),
        in_specs=[SCALAR, pl.BlockSpec((1, 1, 512, 128 * WIDE), lambda t: (h, t, 0, 0)), HBM, HBM]
        + [ANY] * len(held)
        + [HBM] * len(after),
        out_specs=HBM,
        out_shape=shape(16, 256, 128),
        scratch_shapes=[
            pltpu.VMEM((16, *BLOCK), F32),
            pltpu.VMEM((8, 512, 128), F32),
            pltpu.VMEM((8, 512, 128), F32),
            pltpu.VMEM((16, 256, 128), F32),
            pltpu.VMEM((512, 1024), BF16),
            pltpu.VMEM((512, 1024), BF16),
            pltpu.SemaphoreType.DMA((16,)),
            pltpu.SemaphoreType.DMA((2,)),
        ],
        compiler_params=params(),
        cost_estimate=cost(),
    )(me, greater_disp, forward, backward, *held, *after)


def local(lesser, greater, site_of):
    merged = (2, 16, 4, 32, 256)
    me = lax.axis_index("mom").reshape(1)
    greater_out = pack_greater(greater.reshape(merged))
    greater_rows = lax.all_to_all(
        greater_out.reshape(128, 64, 128), ("mom", "tm"), 0, 0, tiled=True
    ).reshape(16, 8, 8, 8, 128)
    sent = pack(me, greater_out, lesser.reshape(merged))
    forward, mirrored, backward = phase_tables(site_of)
    near, far, crossing, disp = exchange(
        sent, (forward,), lambda turned: greater_transform(turned, greater_rows, mirrored)
    )
    far = bubble_transform(1, me, far, disp, forward, backward, (crossing,))
    far = lax.all_to_all(far, "mom", 0, 0, tiled=True).reshape(16, *BLOCK)
    near = bubble_transform(0, me, near, disp, forward, backward)
    near = lax.all_to_all(near, "mom", 0, 0, tiled=True).reshape(16, *BLOCK)
    return unpack(near, unpack(far)).reshape(lesser.shape)


def solution(mesh):
    in_specs = (P(None, "mom", None, None, "tm", None), P(None, "mom", None, None, "tm", None), P())
    out_specs = P(None, "mom", None, None, "tm", None)
    return jax.shard_map(local, mesh=mesh, in_specs=in_specs, out_specs=out_specs, check_vma=False)
```

```python
import functools
import math

import jax
import jax.numpy as jnp
from jax import lax
from jax.experimental import pallas as pl
from jax.experimental.pallas import tpu as pltpu
from jax.sharding import PartitionSpec as P

L = 16
VMEM = 64 * 1024 * 1024 - 384 * 1024
F32 = jnp.float32
BF16 = jnp.bfloat16
BLOCK = (2, 16, 8, 128)
ANY = pl.BlockSpec(memory_space=pl.ANY)
HBM = pl.BlockSpec(memory_space=pltpu.HBM)
SCALAR = pl.BlockSpec(memory_space=pltpu.SMEM)
DISTANCES = [(dz, dx, dc) for dz in range(2) for dx in range(4) for dc in range(2)]


def params():
    return pltpu.CompilerParams(vmem_limit_bytes=VMEM)


def cost():
    return pl.CostEstimate(flops=1, bytes_accessed=1, transcendentals=0)


def shape(*dims):
    return jax.ShapeDtypeStruct(dims, F32)


def split(x):
    high = x.astype(BF16)
    return high, (x - high.astype(F32)).astype(BF16)


def cosines(turns):
    turns = turns % L
    turns = jnp.where(turns > 8, L - turns, turns)
    near = jnp.where(turns > 4, 8 - turns, turns)
    value = jnp.zeros(turns.shape, F32)
    for step in range(4):
        value = jnp.where(near == step, math.cos(2.0 * math.pi * step / L) / L, value)
    return jnp.where(turns > 4, -value, value)


def phase_turns(lattice, site):
    return (lattice // L) * (site // L) + (lattice % L) * (site % L)


def table_body(lesser_ref, greater_ref, result_ref, *outs):
    rows = lax.broadcasted_iota(jnp.int32, (512, 512), 0)
    columns = lax.broadcasted_iota(jnp.int32, (512, 512), 1)
    forward = phase_turns(rows % 256, lesser_ref[...]) + 4 * ((columns // 16) % 2 - rows // 256)
    mirrored = phase_turns(rows % 256, greater_ref[...]) - 4 * ((columns // 4) % 2 - rows // 256)
    backward = phase_turns(columns % 256, result_ref[...]) + 4 * ((rows // 16) % 2 - columns // 256)
    for out, turns in zip(outs, (forward, mirrored, backward)):
        high, low = split(cosines(turns + L))
        out[:, 0:512] = high
        out[:, 512:1024] = low


def phase_tables(site_of):
    parts = jnp.broadcast_to(site_of.reshape(16, 1, 16), (16, 2, 16))
    columns = parts.reshape(512)
    quads = parts.reshape(16, 2, 4, 4).transpose(3, 0, 1, 2).reshape(1, 512)
    return pl.pallas_call(
        table_body,
        out_shape=(jax.ShapeDtypeStruct((512, 1024), BF16),) * 3,
        compiler_params=params(),
        cost_estimate=cost(),
    )(columns.reshape(1, 512), quads, columns.reshape(512, 1))


def times(table_ref, x):
    high, low = split(x)
    table_high, table_low = table_ref[:, 0:512], table_ref[:, 512:1024]
    tables = jnp.concatenate([table_high, table_high, table_low], 1)
    return jnp.dot(tables, jnp.concatenate([high, low, high], 0), preferred_element_type=F32)


def part(ref, m):
    return ref.at[:, :, m // 4, pl.ds(m % 4 * 8, 8), :]


def half(ref, m, h):
    return ref.at[m, :, :, :, pl.ds(128 * h, 128)]


def relay(loads, stores):
    for group in loads:
        for copy in group:
            copy.start()
    for group, after in zip(loads, stores):
        for copy in group:
            copy.wait()
        for copy in after:
            copy.start()
    for group in stores:
        for copy in group:
            copy.wait()


RELAY = [
    pltpu.VMEM((16, 2, 16, 8, 256), F32),
    pltpu.SemaphoreType.DMA((16,)),
    pltpu.SemaphoreType.DMA((16, 2)),
]


def shard_at(me, dz, dx, dc, way):
    x, z, c = me // 4, (me // 2) % 2, me % 2
    return ((x + way * dx + 4) % 4) * 4 + (z + dz) % 2 * 2 + (c + dc) % 2


def moved(values, dz, dx, dc):
    ways = [(m, (m // 4 + dx) % 4 * 4 + (m // 2 + dz) % 2 * 2 + (m + dc) % 2) for m in range(16)]
    return lax.ppermute(values, "mom", ways)


def pack_body(me_ref, after_ref, i_ref, *refs):
    near, far = refs[:2], refs[2:6]
    buffer, one, two = refs[6:]
    copy = pltpu.make_async_copy
    loads, stores = [], []
    for i, (dz, dx, dc) in enumerate(DISTANCES):
        source = part(i_ref, shard_at(me_ref[0], dz, dx, dc, 1))
        loads.append([copy(source, buffer.at[i], one.at[i])])
        stores.append(
            [
                copy(half(buffer, i, 0), near[dz].at[dx, dc], two.at[i, 0]),
                copy(half(buffer, i, 1), far[dx].at[dz, dc], two.at[i, 1]),
            ]
        )
    relay(loads, stores)


def pack(me, after, values):
    return pl.pallas_call(
        pack_body,
        in_specs=[SCALAR, HBM, HBM],
        out_specs=(HBM,) * 6,
        out_shape=(shape(4, 2, *BLOCK),) * 2 + (shape(2, 2, *BLOCK),) * 4,
        scratch_shapes=RELAY,
        compiler_params=params(),
        cost_estimate=cost(),
    )(me, after, values)


def gather(outs, arrays, ready):
    pairs = [(i, j, source) for i, blocks in enumerate(outs) for j, source in enumerate(blocks)]

    def body(*refs):
        made, (buffer, sems) = refs[-2 - len(outs) : -2], refs[-2:]
        copy = pltpu.make_async_copy
        relay(
            [
                [copy(refs[n].at[index], buffer.at[k], sems.at[0, k])]
                for k, (_, _, (n, index)) in enumerate(pairs)
            ],
            [
                [copy(buffer.at[k], made[i].at[j], sems.at[1, k])]
                for k, (i, j, _) in enumerate(pairs)
            ],
        )

    return pl.pallas_call(
        body,
        in_specs=[ANY] * len(arrays) + [HBM] * len(ready),
        out_specs=(HBM,) * len(outs),
        out_shape=tuple(shape(len(blocks), *BLOCK) for blocks in outs),
        scratch_shapes=[
            pltpu.VMEM((len(pairs), *BLOCK), F32),
            pltpu.SemaphoreType.DMA((2, len(pairs))),
        ],
        compiler_params=params(),
        cost_estimate=cost(),
    )(*arrays, *ready)


def exchange(sent, ready, between):
    near = [sent[0], moved(sent[1], 1, 0, 0)]
    far = [sent[2]] + [moved(sent[2 + dx], 0, dx, 0) for dx in range(1, 4)]
    over_z = [[(2 + dx, (1, dc)) for dx in range(4)] for dc in range(2)]
    over_x = [[(dz, (dx, dc)) for dz in range(2) for dc in range(2)] for dx in range(1, 4)]
    turned = gather([*over_z, *over_x], [*near, *far], ready)
    ways = [(1, 0, 0), (1, 0, 1), (0, 1, 0), (0, 2, 0), (0, 3, 0)]
    last = [moved(values, *way) for values, way in zip(turned, ways)]
    near += last[2:5]
    over_core = [
        (1 + dx, 2 * dz + 1) if dx else (dz, (0, 1)) for dz in range(2) for dx in range(4)
    ]
    disp = between(turned[0])
    (beside,) = gather([[(dx, (0, 1)) for dx in range(4)]], far, [disp])
    far = far + last[:2] + [moved(beside, 0, 0, 1)]
    (crossing,) = gather([over_core], near, [disp])
    near.append(moved(crossing, 0, 0, 1))
    return near, far, crossing, disp


def arrived(refs, h, dz, dx, dc):
    if h == 0:
        if dc:
            return refs[5].at[4 * dz + dx]
        return refs[1 + dx].at[2 * dz] if dx else refs[dz].at[0, 0]
    if dz:
        return refs[4 + dc].at[dx]
    return refs[6].at[dx] if dc else refs[dx].at[0, 0]


def unpack_body(*refs):
    i_ref, (o_ref, buffer, one, two) = refs[0], refs[-4:]
    h = 6 - len(refs)
    copy = pltpu.make_async_copy
    relay(
        [[copy(i_ref.at[m], buffer.at[m], one.at[m])] for m in range(16)],
        [
            [copy(buffer.at[m], part(o_ref, m).at[:, :, :, pl.ds(128 * h, 128)], two.at[m])]
            for m in range(16)
        ],
    )


def unpack(values, *done):
    return pl.pallas_call(
        unpack_body,
        in_specs=[ANY] + [HBM] * len(done),
        out_specs=HBM,
        out_shape=shape(2, 16, 4, 32, 256),
        scratch_shapes=[
            pltpu.VMEM((16, *BLOCK), F32),
            pltpu.SemaphoreType.DMA((16,)),
            pltpu.SemaphoreType.DMA((16,)),
        ],
        input_output_aliases={1: 0} if done else {},
        compiler_params=params(),
        cost_estimate=cost(),
    )(values, *done)


def swap_rows(tiles):
    tiles = list(tiles)
    row = lax.broadcasted_iota(jnp.int32, tiles[0].shape, 1)
    for step in (4, 2, 1):
        keep = (row // step) % 2 == 0
        for i in range(8):
            if i // step % 2 == 0:
                a, b = tiles[i], tiles[i + step]
                tiles[i] = jnp.where(keep, a, pltpu.roll(b, step, 1))
                tiles[i + step] = jnp.where(keep, pltpu.roll(a, 8 - step, 1), b)
    return tiles


def pack_greater_body(i_ref, o_ref):
    for h in range(2):
        turned = []
        for c in range(2):
            for q in range(4):
                block = i_ref[c, 4 * q : 4 * q + 4, 0, :, 128 * h : 128 * h + 128]
                turned.append(block.reshape(128, 128).T.reshape(16, 8, 128))
        for t, tile in enumerate(swap_rows(turned)):
            for s in range(4):
                for g in range(4):
                    o_ref[0, g, 4 * h + s, t] = tile[4 * s + g]


def pack_greater(values):
    return pl.pallas_call(
        pack_greater_body,
        grid=(4,),
        in_specs=[
            pl.BlockSpec((2, 16, 1, 32, 256), lambda o: (0, 0, (o % 2) * 2 + o // 2, 0, 0))
        ],
        out_specs=pl.BlockSpec((1, 4, 8, 8, 8, 128), lambda o: (o, 0, 0, 0, 0, 0)),
        out_shape=shape(4, 4, 8, 8, 8, 128),
        compiler_params=params(),
        cost_estimate=cost(),
    )(values)


def swap_blocks(tiles):
    lane = lax.broadcasted_iota(jnp.int32, tiles[0].shape, 1)
    a, b, c, d = tiles
    low = lane < 64
    pairs = []
    for p, q in ((a, c), (b, d)):
        pairs.append(jnp.where(low, p, pltpu.roll(q, 64, 1)))
        pairs.append(jnp.where(low, pltpu.roll(p, 64, 1), q))
    e, f, g, h = pairs[0], pairs[2], pairs[1], pairs[3]
    even = (lane // 32) % 2 == 0
    return (
        jnp.where(even, e, pltpu.roll(f, 32, 1)),
        jnp.where(even, pltpu.roll(e, 96, 1), f),
        jnp.where(even, g, pltpu.roll(h, 32, 1)),
        jnp.where(even, pltpu.roll(g, 96, 1), h),
    )


WIDE = 4


def greater_body(after_ref, x_ref, table_ref, o_ref):
    parts = []
    for i in range(WIDE):
        tiles = [x_ref[:, s, i].reshape(128, 128) for s in range(4)]
        parts.append(jnp.concatenate(swap_blocks(tiles), 0))
    o_ref[0, 0] = times(table_ref, jnp.concatenate(parts, 1))


def greater_transform(after, rows, table):
    steps = 8 // WIDE
    return pl.pallas_call(
        greater_body,
        grid=(2, steps),
        in_specs=[
            HBM,
            pl.BlockSpec((16, 4, WIDE, 8, 128), lambda h, t: (0, h, t, 0, 0)),
            pl.BlockSpec((512, 1024), lambda h, t: (0, 0)),
        ],
        out_specs=pl.BlockSpec((1, 1, 512, 128 * WIDE), lambda h, t: (h, t, 0, 0)),
        out_shape=shape(2, steps, 512, 128 * WIDE),
        compiler_params=params(),
        cost_estimate=cost(),
    )(after, rows, table)


def bubble(lesser, greater):
    lr, li = lesser[0:256], lesser[256:512]
    gr, gi = greater[0:256], greater[256:512]
    return jnp.concatenate([lr * gi + li * gr, li * gi - lr * gr], 0)


def bubble_body(h, me_ref, g_ref, forward_hbm, backward_hbm, *refs):
    held, out_ref, scratch = refs[:-9], refs[-9], refs[-8:]
    rows_ref, turned_ref, result_ref, o_ref, forward_ref, backward_ref, sems, others = scratch
    step = pl.program_id(0)

    @pl.when(step == 0)
    def _():
        tables = [
            pltpu.make_async_copy(forward_hbm, forward_ref, others.at[0]),
            pltpu.make_async_copy(backward_hbm, backward_ref, others.at[1]),
        ]
        shards = [shard_at(me_ref[0], dz, dx, dc, -1) for dz, dx, dc in DISTANCES]
        copies = [
            pltpu.make_async_copy(arrived(held, h, *way), rows_ref.at[i], sems.at[i])
            for i, way in enumerate(DISTANCES)
        ]
        for copy in copies + tables:
            copy.start()
        for i, (copy, shard) in enumerate(zip(copies, shards)):
            copy.wait()
            tiles = rows_ref[i].reshape(4, 8, 8, 128)
            row = pl.multiple_of(32 * shard, 32)
            for t, tile in enumerate(swap_rows([tiles[:, j] for j in range(8)])):
                turned_ref[t, pl.ds(row, 32), :] = tile.reshape(32, 128)
        for copy in tables:
            copy.wait()

    x = jnp.concatenate([turned_ref[WIDE * step + i] for i in range(WIDE)], 1)
    result = times(backward_ref, bubble(times(forward_ref, x), g_ref[0, 0]))
    for i in range(WIDE):
        result_ref[WIDE * step + i] = result[:, 128 * i : 128 * i + 128]

    @pl.when(step == 8 // WIDE - 1)
    def _():
        copies = [pltpu.make_async_copy(o_ref.at[m], out_ref.at[m], sems.at[m]) for m in range(16)]
        for m in range(16):
            tiles = [
                result_ref[t, 32 * m : 32 * m + 32, :].reshape(4, 8, 128) for t in range(8)
            ]
            o_ref[m] = jnp.stack(swap_rows(tiles), 1).reshape(256, 128)
            copies[m].start()
        for copy in copies:
            copy.wait()


def bubble_transform(h, me, held, greater_disp, forward, backward, after=()):
    return pl.pallas_call(
        functools.partial(bubble_body, h),
        grid=(8 // WIDE,),
        in_specs=[SCALAR, pl.BlockSpec((1, 1, 512, 128 * WIDE), lambda t: (h, t, 0, 0)), HBM, HBM]
        + [ANY] * len(held)
        + [HBM] * len(after),
        out_specs=HBM,
        out_shape=shape(16, 256, 128),
        scratch_shapes=[
            pltpu.VMEM((16, *BLOCK), F32),
            pltpu.VMEM((8, 512, 128), F32),
            pltpu.VMEM((8, 512, 128), F32),
            pltpu.VMEM((16, 256, 128), F32),
            pltpu.VMEM((512, 1024), BF16),
            pltpu.VMEM((512, 1024), BF16),
            pltpu.SemaphoreType.DMA((16,)),
            pltpu.SemaphoreType.DMA((2,)),
        ],
        compiler_params=params(),
        cost_estimate=cost(),
    )(me, greater_disp, forward, backward, *held, *after)


def local(lesser, greater, site_of):
    merged = (2, 16, 4, 32, 256)
    me = lax.axis_index("mom").reshape(1)
    greater_out = pack_greater(greater.reshape(merged))
    greater_rows = lax.all_to_all(
        greater_out.reshape(128, 64, 128), ("mom", "tm"), 0, 0, tiled=True
    ).reshape(16, 8, 8, 8, 128)
    sent = pack(me, greater_out, lesser.reshape(merged))
    forward, mirrored, backward = phase_tables(site_of)
    near, far, crossing, disp = exchange(
        sent, (forward,), lambda turned: greater_transform(turned, greater_rows, mirrored)
    )
    far = bubble_transform(1, me, far, disp, forward, backward, (crossing,))
    far = lax.all_to_all(far, "mom", 0, 0, tiled=True).reshape(16, *BLOCK)
    near = bubble_transform(0, me, near, disp, forward, backward)
    near = lax.all_to_all(near, "mom", 0, 0, tiled=True).reshape(16, *BLOCK)
    return unpack(near, unpack(far)).reshape(lesser.shape)


def solution(mesh):
    in_specs = (P(None, "mom", None, None, "tm", None), P(None, "mom", None, None, "tm", None), P())
    out_specs = P(None, "mom", None, None, "tm", None)
    return jax.shard_map(local, mesh=mesh, in_specs=in_specs, out_specs=out_specs, check_vma=False)
```
